32 devices in a mesh: dp: 8 (over y, x, core), tensor: 4 (over z).
Axes of the slice: x: 2, y: 2, z: 4, core: 2. Of those that a mesh axis runs over, the one named last changes fastest.
Arguments:
- tokens: bfloat16 [4096, 1024], P(('dp', 'tensor')), may hold values from -6 to 6
- norm1_gain: float32 [1024], replicated, may hold values from 0.1 to 1.9
- w_query: bfloat16 [1024, 1024], P('dp', 'tensor'), may hold values from -0.1875 to 0.1875
- w_key: bfloat16 [1024, 1024], P('dp', 'tensor'), may hold values from -0.1875 to 0.1875
- w_value: bfloat16 [1024, 2048], P('dp', 'tensor'), may hold values from -0.1875 to 0.1875
- w_gate_out: bfloat16 [1024, 2048], P('dp', 'tensor'), may hold values from -0.1875 to 0.1875
- w_beta: bfloat16 [1024, 8], P('dp', 'tensor'), may hold values from -0.1875 to 0.1875
- w_decay: bfloat16 [1024, 8], P('dp', 'tensor'), may hold values from -0.1875 to 0.1875
- conv_query: float32 [4, 1024], replicated, may hold values from -2.5 to 2.5
- conv_key: float32 [4, 1024], replicated, may hold values from -2.5 to 2.5
- conv_value: float32 [4, 2048], replicated, may hold values from -2.5 to 2.5
- decay_log: float32 [8], replicated, may hold values from 0 to 2.77
- decay_bias: float32 [8], replicated, may hold values from -6.9 to -2.3
- value_gain: float32 [256], replicated, may hold values from 0.1 to 1.9
- w_out: bfloat16 [1024, 2048], P('dp', 'tensor'), may hold values from -0.25 to 0.25
- norm2_gain: float32 [1024], replicated, may hold values from 0.1 to 1.9
- w_gate: bfloat16 [1024, 2816], P('dp', 'tensor'), may hold values from -0.1875 to 0.1875
- w_up: bfloat16 [1024, 2816], P('dp', 'tensor'), may hold values from -0.1875 to 0.1875
- w_down: bfloat16 [1024, 2816], P('dp', 'tensor'), may hold values from -0.21875 to 0.21875
- cotangent: bfloat16 [4096, 1024], P(('dp', 'tensor')), may hold values from -6 to 6
Outputs:
- output: bfloat16 [4096, 1024], P(('dp', 'tensor'))
- grad_tokens: float32 [4096, 1024], P(('dp', 'tensor'))
- grad_norm1_gain: float32 [1024], replicated
- grad_w_query: float32 [1024, 1024], P('dp', 'tensor')
- grad_w_key: float32 [1024, 1024], P('dp', 'tensor')
- grad_w_value: float32 [1024, 2048], P('dp', 'tensor')
- grad_w_gate_out: float32 [1024, 2048], P('dp', 'tensor')
- grad_w_beta: float32 [1024, 8], P('dp', 'tensor')
- grad_w_decay: float32 [1024, 8], P('dp', 'tensor')
- grad_conv_query: float32 [4, 1024], replicated
- grad_conv_key: float32 [4, 1024], replicated
- grad_conv_value: float32 [4, 2048], replicated
- grad_decay_log: float32 [8], replicated
- grad_decay_bias: float32 [8], replicated
- grad_value_gain: float32 [256], replicated
- grad_w_out: float32 [1024, 2048], P('dp', 'tensor')
- grad_norm2_gain: float32 [1024], replicated
- grad_w_gate: float32 [1024, 2816], P('dp', 'tensor')
- grad_w_up: float32 [1024, 2816], P('dp', 'tensor')
- grad_w_down: float32 [1024, 2816], P('dp', 'tensor')
The draws below stay inside these ranges and needn't reach their ends.
All inputs are finite; a program needn't handle non-finite values.
Results may differ from the reference program's by a relative error of at most 0.013.
Values may be sent and summed in bfloat16 or wider, within the bound.
No kernel may reach another device: no remote copies, remote signals or barrier semaphores. Data moves between devices by JAX's collectives and lax.ppermute only.
A program may use at most 192 MiB of HBM per device.

```python
import jax
import jax.numpy as jnp
from jax import lax

D = 1024
HEADS = 8
DK = 128
DV = 256
FF = 2816
CONV = 4
GROUP = 64
KD = 1024
VD = 2048
LENGTH = 1024
SEQS = 4
TOKENS = 4096


def steps_of(rng, extent, split, least, high):
    loudness, own = 1.0, jax.random.fold_in(rng, 6)
    for position, parts in split:
        steps = jnp.exp(jax.random.uniform(jax.random.fold_in(own, position), (parts,), jnp.float32, least / len(split), high / len(split)))
        loudness = loudness * jnp.repeat(steps, extent[position] // parts).reshape([-1 if axis == position else 1 for axis in range(len(extent))])
    return loudness


def gaussian(rng, extent, scale, most, pieces=(), held_as=jnp.bfloat16):
    values = scale * jax.random.normal(rng, extent, jnp.float32)
    if pieces:
        values = values * steps_of(rng, extent, pieces, -0.22, 0.18)
    return jnp.clip(values, -most, most).astype(held_as)


def setup_inputs(seed: int = 0) -> dict:
    keys = jax.random.split(jax.random.key(seed), 21)
    tokens = gaussian(keys[0], (TOKENS, D), 1.0, 6.0, ((0, 32),))
    norm1_gain = jnp.clip(1.0 + 0.18 * jax.random.normal(keys[1], (D,), jnp.float32), 0.1, 1.9)
    w_query = gaussian(keys[2], (D, KD), D ** -0.5, 0.1875, ((0, 8), (1, 4)))
    w_key = gaussian(keys[3], (D, KD), D ** -0.5, 0.1875, ((0, 8), (1, 4)))
    w_value = gaussian(keys[4], (D, VD), D ** -0.5, 0.1875, ((0, 8), (1, 4)))
    w_gate_out = gaussian(keys[5], (D, VD), D ** -0.5, 0.1875, ((0, 8), (1, 4)))
    w_beta = gaussian(keys[6], (D, HEADS), D ** -0.5, 0.1875, ((0, 8), (1, 4)))
    w_decay = gaussian(keys[7], (D, HEADS), D ** -0.5, 0.1875, ((0, 8), (1, 4)))
    conv_query = gaussian(keys[8], (CONV, KD), 0.5, 2.5, (), jnp.float32)
    conv_key = gaussian(keys[9], (CONV, KD), 0.5, 2.5, (), jnp.float32)
    conv_value = gaussian(keys[10], (CONV, VD), 0.5, 2.5, (), jnp.float32)
    decay_log = jnp.clip(jax.random.uniform(keys[11], (HEADS,), jnp.float32, 0.0, 2.77), 0.0, 2.77)
    decay_bias = jnp.clip(jax.random.uniform(keys[12], (HEADS,), jnp.float32, -6.9, -2.3), -6.9, -2.3)
    value_gain = jnp.clip(1.0 + 0.18 * jax.random.normal(keys[13], (DV,), jnp.float32), 0.1, 1.9)
    w_out = gaussian(keys[14], (D, VD), (VD // 4) ** -0.5, 0.25, ((0, 8), (1, 4)))
    norm2_gain = jnp.clip(1.0 + 0.18 * jax.random.normal(keys[15], (D,), jnp.float32), 0.1, 1.9)
    w_gate = gaussian(keys[16], (D, FF), D ** -0.5, 0.1875, ((0, 8), (1, 4)))
    w_up = gaussian(keys[17], (D, FF), D ** -0.5, 0.1875, ((0, 8), (1, 4)))
    w_down = gaussian(keys[18], (D, FF), (FF // 4) ** -0.5, 0.21875, ((0, 8), (1, 4)))
    cotangent = gaussian(keys[19], (TOKENS, D), 1.0, 6.0, ((0, 32),))
    return dict(tokens=tokens, norm1_gain=norm1_gain, w_query=w_query, w_key=w_key, w_value=w_value, w_gate_out=w_gate_out, w_beta=w_beta, w_decay=w_decay, conv_query=conv_query, conv_key=conv_key, conv_value=conv_value, decay_log=decay_log, decay_bias=decay_bias, value_gain=value_gain, w_out=w_out, norm2_gain=norm2_gain, w_gate=w_gate, w_up=w_up, w_down=w_down, cotangent=cotangent)


EPSILON = 1e-06
HIGH = lax.Precision.HIGHEST

@jax.custom_vjp
def low(v):
    return lax.optimization_barrier(v.astype(jnp.bfloat16)).astype(jnp.float32)

@jax.custom_vjp
def low_back(v):
    return v

def low_keep(v):
    return (low(v), None)

def low_pass(kept, grad):
    return (grad,)

def back_keep(v):
    return (v, None)

def back_low(kept, grad):
    return (low(grad),)
low.defvjp(low_keep, low_pass)
low_back.defvjp(back_keep, back_low)

def rms_scale(values, gain):
    return values * lax.rsqrt(lax.optimization_barrier(jnp.mean(values * values, axis=-1, keepdims=True)) + EPSILON) * gain

def short_conv(rim_rows, projected, kernel):
    padded = jnp.concatenate([rim_rows, projected], axis=0)
    length = projected.shape[0]
    total = kernel[0] * padded[0:length]
    for offset in range(1, kernel.shape[0]):
        total = total + kernel[offset] * padded[offset:offset + length]
    return jax.nn.silu(total)

def block_step(state, inputs):
    queries, keys_all, values, betas, decays = inputs
    width = queries.shape[1]
    cumul = jnp.cumsum(decays, axis=1)
    places = jnp.arange(width)
    inclusive = (places[:, None] >= places[None, :]).astype(jnp.float32)
    strictly = (places[:, None] > places[None, :]).astype(jnp.float32)
    spread = cumul[:, :, None] - cumul[:, None, :]
    factors = jnp.exp(jnp.where(inclusive > 0, spread, 0.0)) * inclusive
    key_key = jnp.einsum('hid,hjd->hij', keys_all, keys_all, precision=HIGH)
    system = jnp.eye(width, dtype=jnp.float32) + betas[:, :, None] * factors * key_key * strictly
    growth = jnp.exp(cumul)
    right_side = jnp.concatenate([betas[:, :, None] * values, (betas * growth)[:, :, None] * keys_all], axis=2)
    solved = lax.linalg.triangular_solve(system, right_side, left_side=True, lower=True, unit_diagonal=True)
    value_dim = values.shape[2]
    residual = solved[:, :, :value_dim] - jnp.einsum('hcd,hde->hce', solved[:, :, value_dim:], state, precision=HIGH)
    query_key = jnp.einsum('hid,hjd->hij', queries, keys_all, precision=HIGH) * factors
    outputs = jnp.einsum('hcd,hde->hce', growth[:, :, None] * queries, state, precision=HIGH)
    outputs = outputs + jnp.einsum('hij,hje->hie', query_key, residual, precision=HIGH)
    final = cumul[:, -1]
    tails = jnp.exp(final[:, None] - cumul)
    new_state = jnp.exp(final)[:, None, None] * state + jnp.einsum('hcd,hce->hde', tails[:, :, None] * keys_all, residual, precision=HIGH)
    return (new_state, outputs)

def mixer_core(query_pre, key_pre, value_pre, gate_pre, beta_pre, decay_pre, rim_query, rim_key, rim_value, state, conv_query, conv_key, conv_value, decay_log, decay_bias, value_gain):
    length, heads = beta_pre.shape
    queries = short_conv(rim_query, query_pre, conv_query).reshape(length, heads, -1)
    keys_all = short_conv(rim_key, key_pre, conv_key).reshape(length, heads, -1)
    values = short_conv(rim_value, value_pre, conv_value).reshape(length, heads, -1)
    key_dim = queries.shape[2]
    queries = queries * lax.rsqrt(lax.optimization_barrier(jnp.sum(queries * queries, axis=-1, keepdims=True)) + EPSILON) * key_dim ** (-0.5)
    keys_all = keys_all * lax.rsqrt(lax.optimization_barrier(jnp.sum(keys_all * keys_all, axis=-1, keepdims=True)) + EPSILON)
    betas = jax.nn.sigmoid(beta_pre)
    decays = -jnp.exp(decay_log) * jax.nn.softplus(decay_pre + decay_bias)
    blocks = length // GROUP

    def arrange(array):
        return array.reshape(blocks, GROUP, heads, -1).transpose(0, 2, 1, 3)

    def arrange_flat(array):
        return array.reshape(blocks, GROUP, heads).transpose(0, 2, 1)
    final, outputs = lax.scan(jax.checkpoint(block_step), state, (arrange(queries), arrange(keys_all), arrange(values), arrange_flat(betas), arrange_flat(decays)))
    outputs = outputs.transpose(0, 2, 1, 3).reshape(length, heads, -1)
    outputs = outputs * lax.rsqrt(lax.optimization_barrier(jnp.mean(outputs * outputs, axis=-1, keepdims=True)) + EPSILON) * value_gain
    outputs = outputs * jax.nn.silu(gate_pre.reshape(length, heads, -1))
    return (outputs.reshape(length, -1), final)

def product(left, right):
    return jnp.dot(left.astype(jnp.float32), right.astype(jnp.float32), precision=HIGH, preferred_element_type=jnp.float32)

def product_t(left, right):
    return jnp.dot(left.astype(jnp.float32), right.T.astype(jnp.float32), precision=HIGH, preferred_element_type=jnp.float32)

def block_forward(tokens, norm1_gain, w_query, w_key, w_value, w_gate_out, w_beta, w_decay, conv_query, conv_key, conv_value, decay_log, decay_bias, value_gain, w_out, norm2_gain, w_gate, w_up, w_down):
    normed = low(rms_scale(tokens, norm1_gain))
    query_pre = low_back(product(normed, w_query))
    key_pre = low_back(product(normed, w_key))
    value_pre = low_back(product(normed, w_value))
    gate_pre = low_back(product(normed, w_gate_out))
    beta_pre = low_back(product(normed, w_beta))
    decay_pre = low_back(product(normed, w_decay))
    rim_rows = conv_query.shape[0] - 1
    rim_query = jnp.zeros((rim_rows, w_query.shape[1]), jnp.float32)
    rim_key = jnp.zeros((rim_rows, w_key.shape[1]), jnp.float32)
    rim_value = jnp.zeros((rim_rows, w_value.shape[1]), jnp.float32)
    state = jnp.zeros((HEADS, DK, DV), jnp.float32)
    mixed, final = mixer_core(query_pre, key_pre, value_pre, gate_pre, beta_pre, decay_pre, rim_query, rim_key, rim_value, state, conv_query, conv_key, conv_value, decay_log, decay_bias, value_gain)
    mixed = low(mixed)
    branch = low_back(product_t(mixed, w_out))
    middle = tokens + branch
    normed_two = low(rms_scale(middle, norm2_gain))
    gate_act = low_back(product(normed_two, w_gate))
    up_act = low_back(product(normed_two, w_up))
    hidden = low(jax.nn.silu(gate_act) * up_act)
    return middle + product_t(hidden, w_down)

def reference(tokens, norm1_gain, w_query, w_key, w_value, w_gate_out, w_beta, w_decay, conv_query, conv_key, conv_value, decay_log, decay_bias, value_gain, w_out, norm2_gain, w_gate, w_up, w_down, cotangent):
    params = tuple((array.astype(jnp.float32) for array in (norm1_gain, w_query, w_key, w_value, w_gate_out, w_beta, w_decay, conv_query, conv_key, conv_value, decay_log, decay_bias, value_gain, w_out, norm2_gain, w_gate, w_up, w_down)))
    seq_tokens = tokens.astype(jnp.float32).reshape(SEQS, LENGTH, D)
    seq_cot = cotangent.astype(jnp.float32).reshape(SEQS, LENGTH, D)

    def per_sequence(totals, seq_pair):
        seq_input, seq_grad = seq_pair
        result, pull_back = jax.vjp(block_forward, seq_input, *params)
        grads = pull_back(seq_grad)
        summed = tuple((running + added for running, added in zip(totals, grads[1:])))
        return (summed, (result, grads[0]))
    zeros = tuple((jnp.zeros_like(array) for array in params))
    totals, (results, grad_inputs) = lax.scan(per_sequence, zeros, (seq_tokens, seq_cot))
    return (results.reshape(TOKENS, D).astype(jnp.bfloat16), grad_inputs.reshape(TOKENS, D), totals[0], totals[1], totals[2], totals[3], totals[4], totals[5], totals[6], totals[7], totals[8], totals[9], totals[10], totals[11], totals[12], totals[13], totals[14], totals[15], totals[16], totals[17])
```

```python
import functools
import jax, jax.numpy as jnp
from jax import lax
from jax.experimental import pallas as pl
from jax.experimental.pallas import tpu as pltpu
from jax.sharding import PartitionSpec as P

EPSILON = 1e-06
LANES = 128
CHUNK = 256
SEED = 8
F32 = jnp.float32
BF16 = jnp.bfloat16
NN = (((1,), (0,)), ((), ()))
NT = (((1,), (1,)), ((), ()))
TN = (((0,), (0,)), ((), ()))


def halves(value):
    top = value.astype(BF16)
    return top, (value - top.astype(F32)).astype(BF16)


def dot3(left, right, dims):
    a, b = left if isinstance(left, tuple) else halves(left)
    c, d = right if isinstance(right, tuple) else halves(right)
    run = functools.partial(lax.dot_general, dimension_numbers=dims, preferred_element_type=F32)
    return run(a, c) + (run(a, d) + run(b, c))


def grids(width):
    return (
        lax.broadcasted_iota(jnp.int32, (width, width), 0),
        lax.broadcasted_iota(jnp.int32, (width, width), 1),
    )


def same(rows, columns, size):
    return rows // size == columns // size


def decay_factors(small, row):
    g = small[:, 1:2]
    rows, columns = grids(g.shape[0])
    spread = g - row
    return jnp.where(rows >= columns, jnp.exp(jnp.where(rows >= columns, spread, 0.0)), 0.0), rows, columns


def forward_kernel(chunks, q_ref, k_ref, v_ref, small_ref, row_ref, o_ref, t_ref, s_ref, r_ref):
    width = q_ref.shape[0] // chunks
    systems, inverses, factors = [], [], []
    for c in range(chunks):
        at = slice(c * width, (c + 1) * width)
        small = small_ref[at, :]
        e, rows, columns = decay_factors(small, row_ref[0:1, at])
        k = halves(k_ref[at, :])
        system = jnp.where(rows > columns, small[:, 0:1] * e * dot3(k, k, NT), 0.0)
        systems.append(system)
        factors.append(e)
    seeds = [jnp.where(same(rows, columns, SEED), s, 0.0) for s in systems]
    eye = (rows == columns).astype(F32)
    inverses = [eye - s for s in seeds]
    reach = 2
    while reach < SEED:
        seeds = [halves(s) for s in seeds]
        seeds = [dot3(s, s, NN) for s in seeds]
        inverses = [t + dot3(t, s, NN) for t, s in zip(inverses, seeds)]
        reach *= 2
    size = SEED
    while size < width:
        split = [halves(t) for t in inverses]
        pick = same(rows, columns, 2 * size) & jnp.logical_not(same(rows, columns, size))
        joins = [dot3(jnp.where(pick, s, 0.0), t, NN) for s, t in zip(systems, split)]
        inverses = [t - dot3(p, j, NN) for t, p, j in zip(inverses, split, joins)]
        size *= 2
    state = jnp.zeros((k_ref.shape[1], v_ref.shape[1]), F32)
    for c in range(chunks):
        at = slice(c * width, (c + 1) * width)
        small = small_ref[at, :]
        beta, g = small[:, 0:1], small[:, 1:2]
        growth = jnp.exp(g)
        last = g[width - 1 : width, :]
        tails = jnp.exp(last - g)
        q, k = halves(q_ref[at, :]), halves(k_ref[at, :])
        s_ref[c] = state
        held = halves(state)
        t_ref[c] = inverses[c]
        right = beta * v_ref[at, :] - (beta * growth) * dot3(k, held, NN)
        residual = dot3(inverses[c], right, NN)
        r_ref[at, :] = residual
        both = halves(residual)
        attend = dot3(q, k, NT) * factors[c]
        o_ref[at, :] = growth * dot3(q, held, NN) + dot3(attend, both, NN)
        state = jnp.exp(last) * state + dot3(tails * k_ref[at, :], both, TN)


def backward_kernel(
    chunks, q_ref, k_ref, v_ref, small_ref, row_ref, t_ref, s_ref, r_ref, do_ref,
    dq_ref, dk_ref, dv_ref, dsmall_ref, drow_ref,
):
    width = q_ref.shape[0] // chunks
    dstate = jnp.zeros((k_ref.shape[1], v_ref.shape[1]), F32)
    for c in reversed(range(chunks)):
        at = slice(c * width, (c + 1) * width)
        small = small_ref[at, :]
        beta, g = small[:, 0:1], small[:, 1:2]
        growth = jnp.exp(g)
        last = g[width - 1 : width, :]
        tails = jnp.exp(last - g)
        q_full, k_full = q_ref[at, :], k_ref[at, :]
        q, k = halves(q_full), halves(k_full)
        state = s_ref[c]
        held = halves(state)
        inverse = halves(t_ref[c])
        residual = halves(r_ref[at, :])
        do = halves(do_ref[at, :])
        dnext = halves(dstate)
        e, rows, columns = decay_factors(small, row_ref[0:1, at])
        attend = dot3(q, k, NT) * e
        reach = jnp.where(rows > columns, e * dot3(k, k, NT), 0.0)
        dres = dot3(attend, do, TN) + dot3(tails * k_full, dnext, NN)
        dattend = dot3(do, residual, NT)
        x = dot3(do, held, NT)
        z = dot3(residual, dnext, NT)
        dright_full = dot3(inverse, dres, TN)
        dright = halves(dright_full)
        dsystem = jnp.where(rows > columns, -dot3(dright, residual, NT), 0.0)
        u = dot3(dright, held, NT)
        dqk = halves(dattend * e)
        dkk = halves(dsystem * (beta * e))
        dq_ref[at, :] = growth * x + dot3(dqk, k, NN)
        dk_ref[at, :] = (
            tails * z - (beta * growth) * u + dot3(dqk, q, TN) + dot3(dkk, k, NN) + dot3(dkk, k, TN)
        )
        dv_ref[at, :] = beta * dright_full
        weight = dsystem * reach
        moved = dattend * attend + beta * weight
        along = lambda value: jnp.sum(value, axis=1, keepdims=True)
        uk = along(u * k_full)
        dbeta = along(dright_full * v_ref[at, :]) - growth * uk + along(weight)
        dtail = tails * along(z * k_full)
        dg = along(moved) + growth * (along(x * q_full) - beta * uk) - dtail
        final = jnp.sum(dtail) + jnp.exp(last) * jnp.sum(dstate * state)
        place = lax.broadcasted_iota(jnp.int32, (width, 1), 0)
        dg = dg + jnp.where(place == width - 1, final, 0.0)
        lanes = lax.broadcasted_iota(jnp.int32, (width, dsmall_ref.shape[1]), 1)
        dsmall_ref[at, :] = jnp.where(lanes == 0, dbeta, jnp.where(lanes == 1, dg, 0.0))
        drow_ref[0:1, at] = -jnp.sum(moved, axis=0, keepdims=True)
        dstate = (
            jnp.exp(last) * dstate
            + dot3(growth * q_full, do, TN)
            - dot3((beta * growth) * k_full, dright, TN)
        )


def params():
    return pltpu.CompilerParams(vmem_limit_bytes=56 * 1024 * 1024)


def delta_forward(q, k, v, small, row):
    length, key = q.shape
    value = v.shape[1]
    chunks = length // CHUNK
    shapes = (
        jax.ShapeDtypeStruct((length, value), F32),
        jax.ShapeDtypeStruct((chunks, CHUNK, CHUNK), F32),
        jax.ShapeDtypeStruct((chunks, key, value), F32),
        jax.ShapeDtypeStruct((length, value), F32),
    )
    return pl.pallas_call(
        functools.partial(forward_kernel, chunks),
        out_shape=shapes,
        compiler_params=params(),
        name="delta_forward",
    )(q, k, v, small, row)


def delta_backward(q, k, v, small, row, t, s, r, do):
    length, key = q.shape
    value = v.shape[1]
    chunks = length // CHUNK
    shapes = (
        jax.ShapeDtypeStruct((length, key), F32),
        jax.ShapeDtypeStruct((length, key), F32),
        jax.ShapeDtypeStruct((length, value), F32),
        jax.ShapeDtypeStruct(small.shape, F32),
        jax.ShapeDtypeStruct(row.shape, F32),
    )
    return pl.pallas_call(
        functools.partial(backward_kernel, chunks),
        out_shape=shapes,
        compiler_params=params(),
        name="delta_backward",
    )(q, k, v, small, row, t, s, r, do)


def xor_route(size, step):
    return [(i, i ^ step) for i in range(size)]


def to_xor(block, axis, step):
    return lax.ppermute(block, axis, xor_route(lax.axis_size(axis), step))


def swap_pair(block):
    return to_xor(block, "dp", 1)


def placed(pieces, places):
    rows = pieces[0].shape[0]
    buffer = jnp.zeros((rows * len(pieces),) + pieces[0].shape[1:], pieces[0].dtype)
    for piece, place in zip(pieces, places):
        buffer = lax.dynamic_update_slice_in_dim(buffer, piece, place * rows, 0)
    return buffer


def gather_chips(piece):
    size = lax.axis_size("dp")
    if size > 8:
        groups = [list(range(p, size, 2)) for p in range(2)]
        return lax.all_gather(piece, "dp", axis=0, tiled=True, axis_index_groups=groups)
    chip = lax.axis_index("dp") // 2
    pieces = [piece] + [to_xor(piece, "dp", 2 * s) for s in range(1, size // 2)]
    return placed(pieces, [chip ^ s for s in range(size // 2)])


def scatter_chips(parts):
    size = lax.axis_size("dp")
    low = parts.astype(BF16)
    if size > 8:
        groups = [list(range(p, size, 2)) for p in range(2)]
        return lax.psum_scatter(
            low, "dp", scatter_dimension=0, tiled=False, axis_index_groups=groups
        ).astype(F32)
    chip = lax.axis_index("dp") // 2
    total = lax.dynamic_index_in_dim(parts, chip, 0, False).astype(F32)
    for s in range(1, size // 2):
        sent = lax.dynamic_index_in_dim(low, chip ^ s, 0, False)
        total = total + to_xor(sent, "dp", 2 * s).astype(F32)
    return total


def sum_everywhere(value):
    for axis in ("dp", "tensor"):
        step = 1
        while step < lax.axis_size(axis):
            value = value + to_xor(value, axis, step)
            step *= 2
    return value


def gather_lane(block):
    return [block] + [to_xor(block, "tensor", s) for s in range(1, lax.axis_size("tensor"))]


def scatter_lane(total, parts):
    arrived = [to_xor(part, "tensor", s + 1) for s, part in enumerate(parts)]
    for part in arrived:
        total = total + part.astype(F32)
    return total


def gather_sequence(block):
    lanes = lax.axis_size("tensor")
    lane, half = lax.axis_index("tensor"), lax.axis_index("dp") % 2
    mine = gather_lane(block)
    other = [swap_pair(piece) for piece in mine]
    places = [half * lanes + (lane ^ s) for s in range(lanes)]
    places += [(1 - half) * lanes + (lane ^ s) for s in range(lanes)]
    return placed(mine + other, places)


def scatter_sequence(partial, rows):
    lanes = lax.axis_size("tensor")
    lane, half = lax.axis_index("tensor"), lax.axis_index("dp") % 2
    low = partial.astype(BF16)

    def block(array, side, s):
        return lax.dynamic_slice_in_dim(array, (side * lanes + (lane ^ s)) * rows, rows, 0)

    def joined(s):
        return swap_pair(block(low, 1 - half, s)).astype(F32) + block(low, half, s).astype(F32)

    sent = [joined(s).astype(BF16) for s in range(1, lanes)]
    return scatter_lane(joined(0), sent)


def matmul(left, right, dims=NN):
    return lax.dot_general(left, right, dims, preferred_element_type=F32)


def rms_scale(values, gain):
    return values * lax.rsqrt(jnp.mean(values * values, axis=-1, keepdims=True) + EPSILON) * gain


def short_conv(projected, kernel):
    rim = kernel.shape[0] - 1
    padded = jnp.concatenate([jnp.zeros((rim, projected.shape[1]), F32), projected], axis=0)
    length = projected.shape[0]
    total = kernel[0] * padded[0:length]
    for offset in range(1, kernel.shape[0]):
        total = total + kernel[offset] * padded[offset : offset + length]
    return jax.nn.silu(total)


def unit(values):
    return values * lax.rsqrt(jnp.sum(values * values, axis=-1, keepdims=True) + EPSILON)


@jax.custom_vjp
def delta(q, k, v, small, row):
    return delta_forward(q, k, v, small, row)[0]


def delta_keep(q, k, v, small, row):
    out, inverse, states, residual = delta_forward(q, k, v, small, row)
    return out, (q, k, v, small, row, inverse, states, residual)


def delta_pull(kept, grad):
    return delta_backward(*kept, grad)


delta.defvjp(delta_keep, delta_pull)


def mixer(pre, conv_q, conv_k, conv_v, decay_log, decay_bias, value_gain):
    key, value = conv_q.shape[1], conv_v.shape[1]
    length = pre.shape[0]
    ends = [key, 2 * key, 2 * key + value, 2 * (key + value)]
    q = unit(short_conv(pre[:, : ends[0]], conv_q)) * key ** (-0.5)
    k = unit(short_conv(pre[:, ends[0] : ends[1]], conv_k))
    v = short_conv(pre[:, ends[1] : ends[2]], conv_v)
    gate = pre[:, ends[2] : ends[3]]
    beta = jax.nn.sigmoid(pre[:, ends[3]])
    decays = -jnp.exp(decay_log) * jax.nn.softplus(pre[:, ends[3] + 1] + decay_bias)
    rows, columns = grids(CHUNK)
    upper = (rows <= columns).astype(F32)
    g = jnp.dot(decays.reshape(-1, CHUNK), upper, precision=lax.Precision.HIGHEST).reshape(-1)
    small = jnp.concatenate(
        [beta[:, None], g[:, None], jnp.zeros((length, LANES - 2), F32)], axis=1
    )
    row = jnp.concatenate([g[None, :], jnp.zeros((7, length), F32)], axis=0)
    out = delta(q, k, v, small, row)
    out = rms_scale(out, value_gain)
    return out * jax.nn.silu(gate)


def body(
    tokens, norm1_gain, w_query, w_key, w_value, w_gate_out, w_beta, w_decay,
    conv_query, conv_key, conv_value, decay_log, decay_bias, value_gain,
    w_out, norm2_gain, w_gate, w_up, w_down, cotangent,
):
    lanes = lax.axis_size("tensor")
    chips = lax.axis_size("dp") // 2
    lane, place = lax.axis_index("tensor"), lax.axis_index("dp")
    half = place % 2
    rows = tokens.shape[0]
    slab, width = w_query.shape
    key, value = width // 2, w_value.shape[1] // 2
    hidden_units = w_gate.shape[1]
    head = lane * 2 + half

    def own(array, side, size):
        return lax.dynamic_slice_in_dim(array, side * size, size, 1)

    def mixer_columns(side):
        return jnp.concatenate(
            [
                own(w_query, side, key),
                own(w_key, side, key),
                own(w_value, side, value),
                own(w_gate_out, side, value),
                own(w_beta, side, 1),
                own(w_decay, side, 1),
                jnp.zeros((slab, LANES - 2), BF16),
            ],
            axis=1,
        )

    def by_parity(mine, theirs):
        first = jnp.where(half == 0, mine, theirs)
        return jnp.concatenate([first, jnp.where(half == 0, theirs, mine)], axis=0)

    def gather_heads(columns_of):
        return gather_chips(by_parity(columns_of(half), swap_pair(columns_of(1 - half))))

    def gather_rows(piece):
        mine = gather_chips(piece).reshape(chips, 1, slab, -1)
        theirs = swap_pair(mine)
        ordered = jnp.where(
            half == 0,
            jnp.concatenate([mine, theirs], axis=1),
            jnp.concatenate([theirs, mine], axis=1),
        )
        return ordered.reshape(2 * chips * slab, -1)

    residual_in = tokens.astype(F32)
    normed, norm1_pull = jax.vjp(rms_scale, residual_in, norm1_gain)
    normed_all = gather_sequence(normed.astype(BF16))
    w_mixer = gather_heads(mixer_columns)
    w_out_own = gather_heads(lambda side: own(w_out, side, value))
    cot_all = jnp.concatenate(gather_lane(cotangent), axis=0)
    w_gate_up = gather_rows(jnp.concatenate([w_gate, w_up], axis=1))
    w_down_all = gather_rows(w_down)

    pre = matmul(normed_all, w_mixer)
    conv_q = own(conv_query, head, key)
    conv_k = own(conv_key, head, key)
    conv_v = own(conv_value, head, value)
    log_own = lax.dynamic_slice_in_dim(decay_log, head, 1, 0)
    bias_own = lax.dynamic_slice_in_dim(decay_bias, head, 1, 0)
    mixed, mixer_pull = jax.vjp(
        mixer, pre, conv_q, conv_k, conv_v, log_own, bias_own, value_gain
    )
    mixed_low = mixed.astype(BF16)
    branch = scatter_sequence(matmul(mixed_low, w_out_own, NT), rows)
    middle = residual_in + branch
    normed_two, norm2_pull = jax.vjp(rms_scale, middle, norm2_gain)
    normed_two_all = jnp.concatenate(gather_lane(normed_two.astype(BF16)), axis=0)
    acts = matmul(normed_two_all, w_gate_up)
    gate_act, up_act = acts[:, :hidden_units], acts[:, hidden_units:]
    sigma = jax.nn.sigmoid(gate_act)
    silu_gate = gate_act * sigma
    hidden = (silu_gate * up_act).astype(BF16)
    grad_hidden = matmul(cot_all, w_down_all)
    grad_acts = jnp.concatenate(
        [
            (grad_hidden * up_act * sigma * (1.0 + gate_act * (1.0 - sigma))).astype(BF16),
            (grad_hidden * silu_gate).astype(BF16),
        ],
        axis=1,
    )

    def lane_sum(partial):
        low = partial.astype(BF16)
        pieces = [low[s * rows : (s + 1) * rows] for s in range(lanes)]
        return scatter_lane(pieces[0].astype(F32), pieces[1:])

    grad_normed_two = lane_sum(matmul(grad_acts, w_gate_up, NT))
    output = (middle + lane_sum(matmul(hidden, w_down_all, NT))).astype(BF16)
    grad_middle, grad_norm2_gain = norm2_pull(grad_normed_two)
    grad_middle = grad_middle + cotangent.astype(F32)
    grad_branch_all = gather_sequence(grad_middle.astype(BF16))
    grad_w_gate_up = matmul(normed_two_all, grad_acts, TN)
    grad_w_down = matmul(cot_all, hidden, TN)
    grad_mixed = matmul(grad_branch_all, w_out_own)
    grad_w_out = matmul(grad_branch_all, mixed_low, TN)

    def scatter_rows(partial):
        parts = partial.reshape(chips, 2, slab, -1)
        sent = lax.dynamic_index_in_dim(parts, 1 - half, 1, False).astype(BF16)
        kept = lax.dynamic_index_in_dim(parts, half, 1, False)
        return scatter_chips(kept + swap_pair(sent).astype(F32))

    def scatter_heads(partial):
        total = scatter_chips(partial.reshape(chips, 2 * slab, -1)).reshape(2, slab, -1)
        sent = lax.dynamic_index_in_dim(total, 1 - half, 0, False).astype(BF16)
        mine = lax.dynamic_index_in_dim(total, half, 0, False)
        theirs = swap_pair(sent).astype(F32)
        return jnp.where(half == 0, mine, theirs), jnp.where(half == 0, theirs, mine)

    grad_w_gate_up = scatter_rows(grad_w_gate_up)
    grad_w_down = scatter_rows(grad_w_down)
    grad_w_out = jnp.concatenate(scatter_heads(grad_w_out), axis=1)

    pulled = mixer_pull(grad_mixed)
    grad_pre = pulled[0].astype(BF16)
    grad_normed = scatter_sequence(matmul(grad_pre, w_mixer, NT), rows)
    grad_w_mixer = matmul(normed_all, grad_pre, TN)
    grad_norm1_gain = jnp.sum(grad_w_mixer * w_mixer.astype(F32), axis=1) / norm1_gain
    first, second = scatter_heads(grad_w_mixer)
    ends = [0, key, 2 * key, 2 * key + value, 2 * (key + value)]
    ends = ends + [ends[-1] + 1, ends[-1] + 2]
    mixer_grads = [
        jnp.concatenate([first[:, a:b], second[:, a:b]], axis=1) for a, b in zip(ends, ends[1:])
    ]
    grad_input, _ = norm1_pull(grad_normed)
    grad_tokens = grad_input + grad_middle

    def spread(grad, shape):
        return lax.dynamic_update_slice_in_dim(
            jnp.zeros(shape, F32), grad, head * grad.shape[-1], len(shape) - 1
        )

    parts = [
        grad_norm1_gain,
        spread(pulled[1], conv_query.shape),
        spread(pulled[2], conv_key.shape),
        spread(pulled[3], conv_value.shape),
        spread(pulled[4], decay_log.shape),
        spread(pulled[5], decay_bias.shape),
        pulled[6],
        grad_norm2_gain,
    ]
    flat = jnp.concatenate([part.reshape(-1) for part in parts])
    fill = -flat.shape[0] % (8 * LANES)
    flat = jnp.concatenate([flat, jnp.zeros((fill,), F32)]).reshape(-1, LANES)
    flat = sum_everywhere(flat).reshape(-1)
    sums, start = [], 0
    for part in parts:
        sums.append(flat[start : start + part.size].reshape(part.shape))
        start += part.size
    return (
        output,
        grad_tokens,
        sums[0],
        *mixer_grads,
        *sums[1:7],
        grad_w_out,
        sums[7],
        grad_w_gate_up[:, :hidden_units],
        grad_w_gate_up[:, hidden_units:],
        grad_w_down,
    )


def solution(mesh):
    split, whole, token_rows = P("dp", "tensor"), P(), P(("dp", "tensor"), None)
    return jax.shard_map(
        body,
        mesh=mesh,
        in_specs=(token_rows, whole) + (split,) * 6 + (whole,) * 6
        + (split, whole, split, split, split, token_rows),
        out_specs=(token_rows, token_rows, whole) + (split,) * 6 + (whole,) * 6
        + (split, whole, split, split, split),
        check_vma=False,
    )
```

```python
import functools
import jax, jax.numpy as jnp
from jax import lax
from jax.experimental import pallas as pl
from jax.experimental.pallas import tpu as pltpu
from jax.sharding import PartitionSpec as P

EPSILON = 1e-06
LANES = 128
PAD = 8
CHUNK = 256
SEED = 8
F32 = jnp.float32
BF16 = jnp.bfloat16
NN = (((1,), (0,)), ((), ()))
NT = (((1,), (1,)), ((), ()))
TN = (((0,), (0,)), ((), ()))


def halves(value):
    top = value.astype(BF16)
    return top, (value - top.astype(F32)).astype(BF16)


def dot3(left, right, dims):
    a, b = left if isinstance(left, tuple) else halves(left)
    c, d = right if isinstance(right, tuple) else halves(right)
    run = functools.partial(lax.dot_general, dimension_numbers=dims, preferred_element_type=F32)
    return run(a, c) + (run(a, d) + run(b, c))


def grids(width):
    return (
        lax.broadcasted_iota(jnp.int32, (width, width), 0),
        lax.broadcasted_iota(jnp.int32, (width, width), 1),
    )


def same(rows, columns, size):
    return rows // size == columns // size


def rowwise(value):
    return jnp.sum(value, axis=1, keepdims=True)


def columnwise(value):
    return jnp.sum(value, axis=0, keepdims=True)


def exact_by_ones(left, value, dims):
    top, rest = halves(value)
    last = (value - top.astype(F32) - rest.astype(F32)).astype(BF16)
    run = functools.partial(lax.dot_general, dimension_numbers=dims, preferred_element_type=F32)
    return run(left, top) + (run(left, rest) + run(left, last))


def softplus(value):
    return jnp.maximum(value, 0.0) + jnp.log1p(jnp.exp(-jnp.abs(value)))


def taps_of(pre_ref, start, width, columns, rim):
    return [
        pre_ref[PAD - rim + j + start : PAD - rim + j + start + width, columns]
        for j in range(rim + 1)
    ]


def weighted(taps_ref, values):
    total = taps_ref[0:1, :] * values[0]
    for j in range(1, len(values)):
        total = total + taps_ref[j : j + 1, :] * values[j]
    return total


def unit_scale(values):
    return lax.rsqrt(rowwise(values * values) + EPSILON)


def gates_of(tile, rates_ref, rows, columns):
    beta = jax.nn.sigmoid(tile)[:, 0:1]
    shifted = tile + rates_ref[1:2, :]
    decay = -rates_ref[0:1, :] * softplus(shifted)
    lower = (rows >= columns).astype(BF16)
    total = exact_by_ones(lower, decay, NN)
    row = jnp.transpose(total)[1:2, :]
    return beta, decay, total[:, 1:2], row, shifted


def layout(key, value):
    ends = [0, key, 2 * key, 2 * key + value, 2 * (key + value), 2 * (key + value) + LANES]
    return [slice(a, b) for a, b in zip(ends, ends[1:])]


def forward_kernel(
    block, places_ref, tq_ref, tk_ref, tv_ref, rates_ref, gain_ref, mine_ref, theirs_ref, w_ref,
    mixed_ref, send_ref, keep_ref, pre_ref, t_ref, s_ref, r_ref, o_ref, q_ref, k_ref, v_ref, m_ref,
):
    key, value = tq_ref.shape[1], tv_ref.shape[1]
    rim = tq_ref.shape[0] - 1
    length = o_ref.shape[0]
    width = CHUNK
    chunks = length // width
    blocks = mine_ref.shape[0] // block
    at_q, at_k, at_v, at_gate, at_small = layout(key, value)
    pre_ref[0:PAD, :] = jnp.zeros((PAD, pre_ref.shape[1]), F32)
    span = pre_ref.shape[1]
    first = places_ref[2 * blocks] * (span + value)
    for base, side in ((0, mine_ref), (blocks, theirs_ref)):
        for left in range(0, span, 256):
            size = min(256, span - left)
            own = pl.ds(pl.multiple_of(first + left, LANES), size)
            found = lax.dot_general(side[...], w_ref[:, own], NN, preferred_element_type=F32)
            for s in range(blocks):
                start = pl.multiple_of(PAD + places_ref[base + s] * block, 8)
                pre_ref[pl.ds(start, block), left : left + size] = found[s * block : (s + 1) * block]
    rows, columns = grids(width)
    eye = (rows == columns).astype(F32)
    gates, systems, factors = [], [], []
    for c in range(chunks):
        at = slice(c * width, (c + 1) * width)
        u = weighted(tq_ref, taps_of(pre_ref, c * width, width, at_q, rim))
        u = u * jax.nn.sigmoid(u)
        q_ref[at, :] = u * unit_scale(u) * key ** (-0.5)
        u = weighted(tk_ref, taps_of(pre_ref, c * width, width, at_k, rim))
        u = u * jax.nn.sigmoid(u)
        k_ref[at, :] = u * unit_scale(u)
        u = weighted(tv_ref, taps_of(pre_ref, c * width, width, at_v, rim))
        v_ref[at, :] = u * jax.nn.sigmoid(u)
        tile = pre_ref[PAD + c * width : PAD + (c + 1) * width, at_small]
        beta, _, g, row, _ = gates_of(tile, rates_ref, rows, columns)
        e = jnp.where(rows >= columns, jnp.exp(jnp.where(rows >= columns, g - row, 0.0)), 0.0)
        k = halves(k_ref[at, :])
        systems.append(jnp.where(rows > columns, beta * e * dot3(k, k, NT), 0.0))
        factors.append(e)
        gates.append((beta, g))
    seeds = [jnp.where(same(rows, columns, SEED), s, 0.0) for s in systems]
    inverses = [eye - s for s in seeds]
    reach = 2
    while reach < SEED:
        seeds = [halves(s) for s in seeds]
        seeds = [dot3(s, s, NN) for s in seeds]
        inverses = [t + dot3(t, s, NN) for t, s in zip(inverses, seeds)]
        reach *= 2
    size = SEED
    while size < width:
        split = [halves(t) for t in inverses]
        pick = same(rows, columns, 2 * size) & jnp.logical_not(same(rows, columns, size))
        joins = [dot3(jnp.where(pick, s, 0.0), t, NN) for s, t in zip(systems, split)]
        inverses = [t - dot3(p, j, NN) for t, p, j in zip(inverses, split, joins)]
        size *= 2
    state = jnp.zeros((key, value), F32)
    for c in range(chunks):
        at = slice(c * width, (c + 1) * width)
        beta, g = gates[c]
        growth = jnp.exp(g)
        last = g[width - 1 : width, :]
        tails = jnp.exp(last - g)
        q, k = halves(q_ref[at, :]), halves(k_ref[at, :])
        s_ref[c] = state
        held = halves(state)
        t_ref[c] = inverses[c]
        right = beta * v_ref[at, :] - (beta * growth) * dot3(k, held, NN)
        residual = dot3(inverses[c], right, NN)
        r_ref[at, :] = residual
        both = halves(residual)
        attend = dot3(q, k, NT) * factors[c]
        out = growth * dot3(q, held, NN) + dot3(attend, both, NN)
        o_ref[at, :] = out
        state = jnp.exp(last) * state + dot3(tails * k_ref[at, :], both, TN)
        gate = pre_ref[PAD + c * width : PAD + (c + 1) * width, at_gate]
        scale = lax.rsqrt(rowwise(out * out) * (1.0 / value) + EPSILON)
        m_ref[at, :] = out * scale * gain_ref[0:1, :] * (gate * jax.nn.sigmoid(gate))
    for s in range(2 * blocks):
        start = pl.multiple_of(places_ref[s] * block, 8)
        mixed_ref[s * block : (s + 1) * block, :] = m_ref[pl.ds(start, block), :].astype(BF16)
    side = blocks * block
    w_out = w_ref[:, pl.ds(pl.multiple_of(first + span, LANES), value)]
    run = functools.partial(lax.dot_general, dimension_numbers=NT, preferred_element_type=F32)
    send_ref[...] = run(mixed_ref[side:, :], w_out).astype(BF16)
    keep_ref[...] = run(mixed_ref[:side, :], w_out)


def backward_kernel(
    block, slab, places_ref, tq_ref, tk_ref, tv_ref, rates_ref, gain_ref, mine_ref, theirs_ref, w_ref,
    mixed_ref, pre_ref, t_ref, s_ref, r_ref, o_ref, normed_ref, normed_other_ref,
    send_ref, keep_ref, keep_w_ref, along_ref, gq_ref, gk_ref, gv_ref, misc_ref,
    m_ref, p_ref, uq_ref, uk_ref, uv_ref, grad_ref, dw_ref,
):
    key, value = tq_ref.shape[1], tv_ref.shape[1]
    rim = tq_ref.shape[0] - 1
    length = o_ref.shape[0]
    width = CHUNK
    chunks = length // width
    blocks = mine_ref.shape[0] // block
    at_q, at_k, at_v, at_gate, at_small = layout(key, value)
    span = p_ref.shape[1]
    half = places_ref[2 * blocks]
    first = half * (span + value)
    w_out = pl.ds(pl.multiple_of(first + span, LANES), value)
    for base, side in ((0, mine_ref), (blocks, theirs_ref)):
        found = lax.dot_general(side[...], w_ref[:, w_out], NN, preferred_element_type=F32)
        for s in range(blocks):
            start = pl.multiple_of(places_ref[base + s] * block, 8)
            m_ref[pl.ds(start, block), :] = found[s * block : (s + 1) * block]
    for ref in (uq_ref, uk_ref, uv_ref):
        ref[length : length + PAD, :] = jnp.zeros((PAD, ref.shape[1]), F32)
    for ref in (gq_ref, gk_ref, gv_ref, misc_ref):
        ref[...] = jnp.zeros(ref.shape, F32)
    rows, columns = grids(width)
    place = lax.broadcasted_iota(jnp.int32, (width, 1), 0)
    lanes = lax.broadcasted_iota(jnp.int32, (width, LANES), 1)
    dstate = jnp.zeros((key, value), F32)

    def conv_back(c, u, du, x, taps_ref, held_ref, out_ref, across):
        at = slice(c * width, (c + 1) * width)
        sig = jax.nn.sigmoid(u)
        du = du * sig * (1.0 + u * (1.0 - sig))
        held_ref[at, :] = du
        for j in range(rim + 1):
            out_ref[j : j + 1, :] += columnwise(du * x[j])
        later = [
            held_ref[c * width + rim - j : (c + 1) * width + rim - j, :] for j in range(rim + 1)
        ]
        p_ref[at, across] = weighted(taps_ref, later)

    for c in reversed(range(chunks)):
        at = slice(c * width, (c + 1) * width)
        below = slice(PAD + c * width, PAD + (c + 1) * width)
        x_q = taps_of(pre_ref, c * width, width, at_q, rim)
        x_k = taps_of(pre_ref, c * width, width, at_k, rim)
        x_v = taps_of(pre_ref, c * width, width, at_v, rim)
        u_q, u_k, u_v = weighted(tq_ref, x_q), weighted(tk_ref, x_k), weighted(tv_ref, x_v)
        c_q, c_k, v = u_q * jax.nn.sigmoid(u_q), u_k * jax.nn.sigmoid(u_k), u_v * jax.nn.sigmoid(u_v)
        inv_q, inv_k = unit_scale(c_q) * key ** (-0.5), unit_scale(c_k)
        q_full, k_full = c_q * inv_q, c_k * inv_k
        beta, decay, g, row, shifted = gates_of(pre_ref[below, at_small], rates_ref, rows, columns)
        e = jnp.where(rows >= columns, jnp.exp(jnp.where(rows >= columns, g - row, 0.0)), 0.0)
        out, gate, dmixed = o_ref[at, :], pre_ref[below, at_gate], m_ref[at, :]
        scale = lax.rsqrt(rowwise(out * out) * (1.0 / value) + EPSILON)
        plain = out * scale
        sig = jax.nn.sigmoid(gate)
        dnormed = dmixed * gate * sig
        p_ref[at, at_gate] = (
            dmixed * plain * gain_ref[0:1, :] * sig * (1.0 + gate * (1.0 - sig))
        )
        misc_ref[0:1, :] += columnwise(dnormed * plain)
        dplain = dnormed * gain_ref[0:1, :]
        dout = scale * (dplain - plain * (rowwise(dplain * plain) * (1.0 / value)))
        growth = jnp.exp(g)
        last = g[width - 1 : width, :]
        tails = jnp.exp(last - g)
        q, k = halves(q_full), halves(k_full)
        state = s_ref[c]
        held = halves(state)
        inverse = halves(t_ref[c])
        residual = halves(r_ref[at, :])
        do = halves(dout)
        dnext = halves(dstate)
        attend = dot3(q, k, NT) * e
        reach = jnp.where(rows > columns, e * dot3(k, k, NT), 0.0)
        dres = dot3(attend, do, TN) + dot3(tails * k_full, dnext, NN)
        dattend = dot3(do, residual, NT)
        x = dot3(do, held, NT)
        z = dot3(residual, dnext, NT)
        dright_full = dot3(inverse, dres, TN)
        dright = halves(dright_full)
        dsystem = jnp.where(rows > columns, -dot3(dright, residual, NT), 0.0)
        u = dot3(dright, held, NT)
        dqk = halves(dattend * e)
        dkk = halves(dsystem * (beta * e))
        dq = growth * x + dot3(dqk, k, NN)
        dk = tails * z - (beta * growth) * u + dot3(dqk, q, TN) + dot3(dkk, k, NN) + dot3(dkk, k, TN)
        weight = dsystem * reach
        moved = dattend * attend + beta * weight
        uk = rowwise(u * k_full)
        dbeta = rowwise(dright_full * v) - growth * uk + rowwise(weight)
        dtail = tails * rowwise(z * k_full)
        dg = rowwise(moved) + growth * (rowwise(x * q_full) - beta * uk) - dtail
        final = jnp.sum(dtail) + jnp.exp(last) * jnp.sum(dstate * state)
        dg = dg + jnp.where(place == width - 1, final, 0.0)
        dg = dg - jnp.transpose(jnp.broadcast_to(columnwise(moved), (LANES, width)))
        upper = (rows <= columns).astype(BF16)
        ddecay = exact_by_ones(upper, dg, NN)
        dstate = (
            jnp.exp(last) * dstate
            + dot3(growth * q_full, do, TN)
            - dot3((beta * growth) * k_full, dright, TN)
        )
        dshifted = -ddecay * rates_ref[0:1, :] * jax.nn.sigmoid(shifted)
        p_ref[at, at_small] = jnp.where(
            lanes == 0, dbeta * beta * (1.0 - beta), jnp.where(lanes == 1, dshifted, 0.0)
        )
        misc_ref[1:2, 0:LANES] += columnwise(ddecay * decay)
        misc_ref[2:3, 0:LANES] += columnwise(dshifted)
        dc_q = inv_q * (dq - q_full * (rowwise(dq * q_full) * key))
        dc_k = inv_k * (dk - k_full * rowwise(dk * k_full))
        conv_back(c, u_q, dc_q, x_q, tq_ref, uq_ref, gq_ref, at_q)
        conv_back(c, u_k, dc_k, x_k, tk_ref, uk_ref, gk_ref, at_k)
        conv_back(c, u_v, beta * dright_full, x_v, tv_ref, uv_ref, gv_ref, at_v)
    for s in range(2 * blocks):
        start = pl.multiple_of(places_ref[s] * block, 8)
        grad_ref[s * block : (s + 1) * block, :] = p_ref[pl.ds(start, block), :].astype(BF16)
    side = blocks * block
    wide = w_ref.shape[0]
    run = functools.partial(lax.dot_general, preferred_element_type=F32)
    w_own = w_ref[:, pl.ds(pl.multiple_of(first, LANES), span)]
    send_ref[:, :wide] = run(grad_ref[side:, :], w_own, NT).astype(BF16)
    keep_ref[...] = run(grad_ref[:side, :], w_own, NT)
    dw = run(normed_ref[...], grad_ref[:side, :], TN) + run(
        normed_other_ref[...], grad_ref[side:, :], TN
    )
    along_ref[...] = rowwise(dw * w_own.astype(F32))
    dw_ref[:, :span] = dw
    dw_ref[:, span:] = run(mine_ref[...], mixed_ref[:side, :], TN) + run(
        theirs_ref[...], mixed_ref[side:, :], TN
    )
    for c in range(wide // (2 * slab)):
        here = pl.ds(pl.multiple_of((2 * c + half) * slab, 8), slab)
        there = pl.ds(pl.multiple_of((2 * c + 1 - half) * slab, 8), slab)
        keep_w_ref[c * slab : (c + 1) * slab, :] = dw_ref[here, :]
        send_ref[c * slab : (c + 1) * slab, wide:] = dw_ref[there, :].astype(BF16)


def call(kernel, name, operands, shapes, scratch, flops):
    specs = [pl.BlockSpec(memory_space=pltpu.SMEM)]
    specs += [pl.BlockSpec(memory_space=pltpu.VMEM)] * (len(operands) - 1)
    moved = sum(a.size * a.dtype.itemsize for a in list(operands) + list(shapes))
    return pl.pallas_call(
        kernel,
        in_specs=specs,
        out_specs=tuple(pl.BlockSpec(memory_space=pltpu.VMEM) for _ in shapes),
        out_shape=tuple(shapes),
        scratch_shapes=scratch,
        compiler_params=pltpu.CompilerParams(vmem_limit_bytes=56 * 1024 * 1024),
        cost_estimate=pl.CostEstimate(flops=flops, bytes_accessed=moved, transcendentals=0),
        name=name,
    )(*operands)


def mixer_forward(places, taps_q, taps_k, taps_v, rates, gain, mine, theirs, w, block):
    side = mine.shape[0]
    length = 2 * side
    key, value = taps_q.shape[1], taps_v.shape[1]
    chunks = length // CHUNK
    full = jax.ShapeDtypeStruct((length, value), F32)
    shapes = (
        jax.ShapeDtypeStruct((length, value), BF16),
        jax.ShapeDtypeStruct((side, w.shape[0]), BF16),
        jax.ShapeDtypeStruct((side, w.shape[0]), F32),
        jax.ShapeDtypeStruct((length + PAD, w.shape[1] // 2 - value), F32),
        jax.ShapeDtypeStruct((chunks, CHUNK, CHUNK), F32),
        jax.ShapeDtypeStruct((chunks, key, value), F32),
        full,
        full,
    )
    scratch = [pltpu.VMEM((length, key), F32)] * 2 + [pltpu.VMEM((length, value), F32)] * 2
    return call(
        functools.partial(forward_kernel, block), "mixer_forward",
        (places, taps_q, taps_k, taps_v, rates, gain, mine, theirs, w), shapes, scratch, 2 * 10**10,
    )


def mixer_backward(
    places, taps_q, taps_k, taps_v, rates, gain, mine, theirs, w, kept, normed, normed_other, block, slab
):
    side, wide = mine.shape
    length = 2 * side
    key, value = taps_q.shape[1], taps_v.shape[1]
    span = kept[1].shape[1]
    shapes = (
        jax.ShapeDtypeStruct((side, wide + span + value), BF16),
        jax.ShapeDtypeStruct((side, wide), F32),
        jax.ShapeDtypeStruct((wide // 2, span + value), F32),
        jax.ShapeDtypeStruct((wide, 1), F32),
        jax.ShapeDtypeStruct((8, key), F32),
        jax.ShapeDtypeStruct((8, key), F32),
        jax.ShapeDtypeStruct((8, value), F32),
        jax.ShapeDtypeStruct((8, value), F32),
    )
    scratch = [
        pltpu.VMEM((length, value), F32),
        pltpu.VMEM((length, span), F32),
        pltpu.VMEM((length + PAD, key), F32),
        pltpu.VMEM((length + PAD, key), F32),
        pltpu.VMEM((length + PAD, value), F32),
        pltpu.VMEM((length, span), BF16),
        pltpu.VMEM((wide, span + value), F32),
    ]
    return call(
        functools.partial(backward_kernel, block, slab), "mixer_backward",
        (places, taps_q, taps_k, taps_v, rates, gain, mine, theirs, w) + tuple(kept)
        + (normed, normed_other),
        shapes, scratch, 2 * 10**10,
    )


def xor_route(size, step):
    return [(i, i ^ step) for i in range(size)]


def to_xor(block, axis, step):
    return lax.ppermute(block, axis, xor_route(lax.axis_size(axis), step))


def swap_pair(block):
    return to_xor(block, "dp", 1)


def parity_groups(size):
    return [list(range(p, size, 2)) for p in range(2)]


def chips_exchange(both, extra, slab):
    size = lax.axis_size("dp")
    chip = lax.axis_index("dp") // 2
    return [
        to_xor(
            jnp.concatenate(
                [lax.dynamic_slice_in_dim(both, (chip ^ s) * slab, slab, 0), extra], axis=0
            ),
            "dp",
            2 * s,
        )
        for s in range(1, size // 2)
    ]


def chips_sum(both, extra, slab):
    groups = parity_groups(lax.axis_size("dp"))
    own = lax.dynamic_slice_in_dim(both, lax.axis_index("dp") // 2 * slab, slab, 0).astype(F32)
    total = lax.psum_scatter(both, "dp", scatter_dimension=0, tiled=True, axis_index_groups=groups)
    others = (total.astype(F32) - own).astype(BF16)
    return others, lax.psum(extra.astype(F32), "dp", axis_index_groups=groups)


def sum_sequence(value):
    hops = [("dp", 1)]
    step = 1
    while step < lax.axis_size("tensor"):
        hops.append(("tensor", step))
        step *= 2
    for axis, step in hops:
        value = value + to_xor(value, axis, step)
    return value


def gather_lane(block):
    pieces = [block] + [to_xor(block, "tensor", s) for s in range(1, lax.axis_size("tensor"))]
    return jnp.concatenate(pieces, axis=0)


def exchange_lane(low, rows):
    lanes = lax.axis_size("tensor")
    return [to_xor(low[s * rows : (s + 1) * rows], "tensor", s) for s in range(1, lanes)]


def add_all(total, pieces):
    for piece in pieces:
        total = total + piece.astype(F32)
    return total


def tie(value, *others):
    return pl.pallas_call(
        lambda *refs: None,
        in_specs=[pl.BlockSpec(memory_space=pl.ANY)] * (1 + len(others)),
        out_specs=pl.BlockSpec(memory_space=pl.ANY),
        out_shape=jax.ShapeDtypeStruct(value.shape, value.dtype),
        input_output_aliases={0: 0},
        name="tie",
    )(value, *others)


def matmul(left, right, dims=NN):
    return lax.dot_general(left, right, dims, preferred_element_type=F32)


def feed_kernel(
    rows, n_ref, c_ref, w_ref, grad_ref, grad_low_ref, out_ref, out_low_ref, hidden_ref, acts_ref
):
    units = hidden_ref.shape[1]
    run = functools.partial(lax.dot_general, preferred_element_type=F32)
    gate = run(n_ref[...], w_ref[:, :units], NN)
    up = run(n_ref[...], w_ref[:, units : 2 * units], NN)
    back = run(c_ref[...], w_ref[:, 2 * units :], NN)
    sig = jax.nn.sigmoid(gate)
    silu = gate * sig
    hidden_ref[...] = (silu * up).astype(BF16)
    acts_ref[:, :units] = (back * up * sig * (1.0 + gate * (1.0 - sig))).astype(BF16)
    acts_ref[:, units:] = (back * silu).astype(BF16)
    total = run(acts_ref[...], w_ref[:, : 2 * units], NT)
    grad_ref[...] = total[:rows]
    grad_low_ref[...] = total.astype(BF16)
    total = run(hidden_ref[...], w_ref[:, 2 * units :], NT)
    out_ref[...] = total[:rows]
    out_low_ref[...] = total.astype(BF16)


def feed(normed, cotangent, w, rows):
    side, wide = normed.shape
    units = w.shape[1] // 3
    vmem = pl.BlockSpec(memory_space=pltpu.VMEM)
    shapes = []
    for _ in range(2):
        shapes += [jax.ShapeDtypeStruct((rows, wide), F32), jax.ShapeDtypeStruct((side, wide), BF16)]
    shapes += [jax.ShapeDtypeStruct((side, units), BF16), jax.ShapeDtypeStruct((side, 2 * units), BF16)]
    return pl.pallas_call(
        functools.partial(feed_kernel, rows),
        in_specs=[vmem] * 3,
        out_specs=(vmem,) * 6,
        out_shape=tuple(shapes),
        compiler_params=pltpu.CompilerParams(vmem_limit_bytes=48 * 1024 * 1024),
        cost_estimate=pl.CostEstimate(
            flops=12 * side * wide * units, bytes_accessed=12 * 2**20, transcendentals=0
        ),
        name="feed",
    )(normed, cotangent, w)


def finish_kernel(key, value, lanes, moved, half_ref, here_ref, there_ref, part_ref, *refs):
    arrived, (tokens_ref, gain_ref, middle_ref) = refs[: lanes - 1], refs[lanes - 1 : lanes + 2]
    out_ref, q_ref, k_ref, v_ref, gate_ref, beta_ref, decay_ref, w_ref = refs[-8:]
    chips = refs[lanes + 2 : lanes + 2 + moved]
    total = part_ref[...]
    for ref in arrived:
        total = total + ref[...].astype(F32)
    x = tokens_ref[...].astype(F32)
    scale = lax.rsqrt(rowwise(x * x) * (1.0 / x.shape[1]) + EPSILON)
    plain = x * scale
    grad = total * gain_ref[0:1, :]
    back = scale * (grad - plain * (rowwise(grad * plain) * (1.0 / x.shape[1])))
    out_ref[...] = back + middle_ref[...]
    first = half_ref[0] == 0
    slab, span = here_ref.shape
    start = 0
    wide = ((q_ref, key), (k_ref, key), (v_ref, value), (gate_ref, value), (None, LANES), (w_ref, value))
    for ref, size in wide:
        here = here_ref[:, start : start + size]
        there = there_ref[:, start : start + size].astype(F32)
        for chip in chips:
            here = here + chip[:slab, start : start + size].astype(F32)
            there = there + chip[:slab, span + start : span + start + size].astype(F32)
        left, right = jnp.where(first, here, there), jnp.where(first, there, here)
        if ref is None:
            left, right = jnp.transpose(left), jnp.transpose(right)
            for lane, out in enumerate((beta_ref, decay_ref)):
                out[0:1, :] = left[lane : lane + 1, :]
                out[1:2, :] = right[lane : lane + 1, :]
        else:
            ref[:, :size] = left
            ref[:, size:] = right
        start += size


def finish(half, here, there, part, arrived, tokens, gain, middle, chips, key, value, others):
    slab = here.shape[0]
    inner = (here, there, part, *arrived, tokens, gain, middle, *chips)
    shapes = [jax.ShapeDtypeStruct(part.shape, F32)]
    shapes += [jax.ShapeDtypeStruct((slab, 2 * size), F32) for size in (key, key, value, value)]
    shapes += [jax.ShapeDtypeStruct((2, slab), F32)] * 2
    shapes += [jax.ShapeDtypeStruct((slab, 2 * value), F32)]
    vmem = pl.BlockSpec(memory_space=pltpu.VMEM)
    return pl.pallas_call(
        functools.partial(finish_kernel, key, value, len(arrived) + 1, len(chips)),
        in_specs=[pl.BlockSpec(memory_space=pltpu.SMEM)]
        + [vmem] * len(inner)
        + [pl.BlockSpec(memory_space=pl.ANY)] * len(others),
        out_specs=tuple(vmem for _ in shapes),
        out_shape=tuple(shapes),
        compiler_params=pltpu.CompilerParams(vmem_limit_bytes=16 * 1024 * 1024),
        name="finish",
    )(half, *inner, *others)


def rms_scale(values, gain):
    return values * lax.rsqrt(jnp.mean(values * values, axis=-1, keepdims=True) + EPSILON) * gain


def body(
    tokens, norm1_gain, w_query, w_key, w_value, w_gate_out, w_beta, w_decay,
    conv_query, conv_key, conv_value, decay_log, decay_bias, value_gain,
    w_out, norm2_gain, w_gate, w_up, w_down, cotangent,
):
    lanes = lax.axis_size("tensor")
    chips = lax.axis_size("dp") // 2
    lane, half = lax.axis_index("tensor"), lax.axis_index("dp") % 2
    rows = tokens.shape[0]
    slab, width = w_query.shape
    key, value = width // 2, w_value.shape[1] // 2
    units = w_gate.shape[1]
    head = lane * 2 + half
    order = [lane ^ s for s in range(lanes)]
    places = jnp.stack(
        [half * lanes + o for o in order] + [(1 - half) * lanes + o for o in order] + [half]
    ).astype(jnp.int32)

    def own(array, side, size):
        return lax.dynamic_slice_in_dim(array, side * size, size, 1)

    def columns_of(array, side):
        size = array.shape[1] // 2
        return array[:, side * size : (side + 1) * size]

    def mixer_columns(side):
        return jnp.concatenate(
            [
                *(columns_of(w, side) for w in (w_query, w_key, w_value, w_gate_out, w_beta, w_decay)),
                jnp.zeros((slab, LANES - 2), BF16),
                columns_of(w_out, side),
            ],
            axis=1,
        )

    residual_in = tokens.astype(F32)
    w_mixer = lax.all_gather(
        jnp.concatenate([mixer_columns(0), mixer_columns(1)], axis=1), "dp", axis=0, tiled=True
    )
    normed = rms_scale(residual_in, norm1_gain)
    mine = gather_lane(normed.astype(BF16))
    theirs = swap_pair(mine)
    cot_early = tie(cotangent, mine)
    cot_arrived = [to_xor(cot_early, "tensor", s) for s in range(1, lanes)]
    units_held = units + -units % LANES
    w_ff = lax.all_gather(
        tie(
            jnp.concatenate(
                [jnp.pad(w, ((0, 0), (0, units_held - units))) for w in (w_gate, w_up, w_down)], axis=1
            ),
            mine,
        ),
        "dp",
        axis=0,
        tiled=True,
    )

    taps = (own(conv_query, head, key), own(conv_key, head, key), own(conv_value, head, value))
    log_own = lax.dynamic_slice_in_dim(decay_log, head, 1, 0)
    bias_own = lax.dynamic_slice_in_dim(decay_bias, head, 1, 0)
    rates = jnp.concatenate(
        [
            jnp.broadcast_to(jnp.exp(log_own)[:, None], (1, LANES)),
            jnp.broadcast_to(bias_own[:, None], (1, LANES)),
            jnp.zeros((6, LANES), F32),
        ],
        axis=0,
    )
    gain = value_gain[None, :]
    mixed, sent, held, *kept = mixer_forward(
        places, *taps, rates, gain, mine, theirs, w_mixer, rows
    )
    cot_all = jnp.concatenate([cotangent, *cot_arrived], axis=0)
    summed = held + swap_pair(tie(sent, tie(tie(rates, sent), *cot_arrived))).astype(F32)
    middle = residual_in + add_all(summed[:rows], exchange_lane(summed.astype(BF16), rows))
    normed_two, norm2_pull = jax.vjp(rms_scale, middle, norm2_gain)
    normed_two_all = gather_lane(normed_two.astype(BF16))
    grad_part, grad_low, out_part, out_low, hidden, grad_acts = feed(
        normed_two_all, cot_all, w_ff, rows
    )
    grad_arrived = exchange_lane(grad_low, rows)
    grad_w_ff = jnp.concatenate(
        [matmul(normed_two_all, grad_acts, TN), matmul(cot_all, hidden, TN)], axis=1
    ).astype(BF16)
    grad_normed_two = add_all(tie(grad_part, grad_w_ff), grad_arrived)
    grad_middle, grad_norm2_gain = norm2_pull(grad_normed_two)
    grad_middle = grad_middle + cotangent.astype(F32)
    mine_grad = gather_lane(grad_middle.astype(BF16))
    theirs_grad = swap_pair(mine_grad)
    grad_w_ff = lax.psum_scatter(grad_w_ff, "dp", scatter_dimension=0, tiled=True).astype(F32)
    grads_ff = tuple(grad_w_ff[:, i * units_held : i * units_held + units] for i in range(3))
    out_arrived = exchange_lane(tie(out_low, mine_grad), rows)
    sent, held, held_w, along, *sums = mixer_backward(
        places, *taps, rates, gain, mine_grad, theirs_grad, w_mixer, (mixed, *kept), mine, theirs,
        rows, slab,
    )
    output = add_all(tie(middle, sent) + out_part, out_arrived).astype(BF16)
    got = swap_pair(tie(sent, output))
    wide = middle.shape[1]
    summed = held + got[:, :wide].astype(F32)
    part, arrived = summed[:rows], exchange_lane(summed.astype(BF16), rows)
    got_w = got[:, wide:]
    chip = lax.axis_index("dp") // 2
    grad_norm1_gain = along[:, 0] / norm1_gain
    def spread(grad, shape):
        return lax.dynamic_update_slice_in_dim(
            jnp.zeros(shape, F32), grad, head * grad.shape[-1], len(shape) - 1
        )

    taps_held = conv_query.shape[0]
    parts = [
        grad_norm1_gain,
        spread(sums[0][:taps_held], conv_query.shape),
        spread(sums[1][:taps_held], conv_key.shape),
        spread(sums[2][:taps_held], conv_value.shape),
        spread(sums[3][1, 1:2], decay_log.shape),
        spread(sums[3][2, 1:2], decay_bias.shape),
        sums[3][0],
        grad_norm2_gain,
    ]
    flat = jnp.concatenate([share.reshape(-1) for share in parts])
    across = 2 * held_w.shape[1]
    fill = -flat.shape[0] % (16 * across)
    fill_lanes = -flat.shape[0] % (8 * LANES)
    flat = jnp.concatenate([flat, jnp.zeros((fill_lanes,), F32)]).reshape(-1, LANES)
    flat = sum_sequence(flat).reshape(-1).astype(BF16)
    extra = jnp.concatenate([flat, jnp.zeros((fill - fill_lanes,), BF16)]).reshape(-1, across)
    extra = tie(extra, output)
    both = jnp.concatenate([held_w.astype(BF16), got_w], axis=1)
    if chips > 4:
        others, flat = chips_sum(both, extra, slab)
        from_chips = [others]
    else:
        from_chips = chips_exchange(both, extra, slab)
        low = [extra.astype(F32)] + [piece[slab:].astype(F32) for piece in from_chips]
        while len(low) > 1:
            low = [a + b for a, b in zip(low[::2], low[1::2])]
        flat = low[0]
    flat = flat.reshape(-1)
    small, start = [], 0
    for share in parts:
        small.append(flat[start : start + share.size].reshape(share.shape))
        start += share.size
    here = lax.dynamic_slice_in_dim(held_w, chip * slab, slab, 0)
    there = lax.dynamic_slice_in_dim(got_w, chip * slab, slab, 0)
    (
        grad_tokens, grad_w_query, grad_w_key, grad_w_value, grad_w_gate_out, grad_w_beta,
        grad_w_decay, grad_w_out,
    ) = finish(
        half[None].astype(jnp.int32), here, there, part, arrived, tokens, norm1_gain[None, :],
        grad_middle, from_chips, key, value, grads_ff,
    )

    return (
        output,
        grad_tokens,
        small[0],
        grad_w_query,
        grad_w_key,
        grad_w_value,
        grad_w_gate_out,
        grad_w_beta.T,
        grad_w_decay.T,
        *small[1:7],
        grad_w_out,
        small[7],
        *grads_ff,
    )


def solution(mesh):
    split, whole, token_rows = P("dp", "tensor"), P(), P(("dp", "tensor"), None)
    return jax.shard_map(
        body,
        mesh=mesh,
        in_specs=(token_rows, whole) + (split,) * 6 + (whole,) * 6
        + (split, whole, split, split, split, token_rows),
        out_specs=(token_rows, token_rows, whole) + (split,) * 6 + (whole,) * 6
        + (split, whole, split, split, split),
        check_vma=False,
    )
```
